32 devices in a mesh: tm: 4 (over y, x), tile: 8 (over z, core).
Axes of the slice: x: 2, y: 2, z: 4, core: 2. Of those that a mesh axis runs over, the one named last changes fastest.
Arguments:
- latent: bfloat16 [16, 32, 32, 256], P('tm', 'tile'), may hold values from -6 to 6
- tile_rows: int32 [8], replicated, may hold values from 1 to 4, 16 in all
- kernel_one: bfloat16 [3, 3, 3, 256, 256], replicated, may hold values from -0.078125 to 0.078125
- bias_one: float32 [256], replicated, may hold values from -3 to 3
- kernel_two: bfloat16 [3, 3, 3, 256, 256], replicated, may hold values from -0.078125 to 0.078125
- bias_two: float32 [256], replicated, may hold values from -3 to 3
Outputs:
- frames_out: bfloat16 [16, 64, 64, 256], P('tm', 'tile')
The draws below stay inside these ranges and needn't reach their ends.
Inputs may be any that keep to these rules, and one draw needn't show every extreme that they name: `tile_rows`: each tile has 1 to 4 rows, they sum to 16, and some tile has exactly 4.
All inputs are finite; a program needn't handle non-finite values.
Results may differ from the reference program's by a relative error of at most 0.0031.
Values may be sent and summed in bfloat16 or wider, within the bound.
No kernel may reach another device: no remote copies, remote signals or barrier semaphores. Data moves between devices by JAX's collectives and lax.ppermute only.
A program may use at most 64 MiB of HBM per device.

```python
import math
import jax
import jax.numpy as jnp
import numpy as np
from jax import lax

CHANNELS = 256
ROW_CAP = 4
LAT_COLS = 32
FRAMES = 16
TOTAL_ROWS = 16
N_TILE = 8


def block_levels(own_key, shape, split, least, top_value):
    loudness, own = 1.0, jax.random.fold_in(own_key, 6)
    for dim, parts in split:
        draws = jnp.exp(jax.random.uniform(jax.random.fold_in(own, dim), (parts,), jnp.float32, least / len(split), top_value / len(split)))
        loudness = loudness * jnp.repeat(draws, shape[dim] // parts).reshape([-1 if axis == dim else 1 for axis in range(len(shape))])
    return loudness


def profile(count, total, bound, skew):
    weights = [(1 << 20) // math.isqrt(grade ** skew) + 1 for grade in range(2, count + 1)]
    rest, counts = total - bound - (count - 1), [1] * (count - 1)
    while rest > 0:
        free = [i for i in range(count - 1) if counts[i] < bound]
        whole, budget = sum([weights[i] for i in free]), rest
        for i in free:
            extra = min(bound - counts[i], max(1, budget * weights[i] // whole), rest)
            counts[i] = counts[i] + extra
            rest = rest - extra
    return np.array([bound] + counts)


def uneven(key, count, total, limit, skew):
    if count == 2:
        one = jax.random.randint(key, (), max(1, total - limit), min(limit, total - 1) + 1)
        return jnp.stack([one, total - one])
    sizes = jnp.asarray(profile(count, total, limit, skew), jnp.int32)
    twos = (count - 1) // 2
    source_of, receiver = sizes[1:1 + 2 * twos:2], sizes[2:2 + 2 * twos:2]
    room = jnp.minimum(source_of - 1, limit - receiver)
    shifted = jax.random.randint(jax.random.fold_in(key, 1), (twos,), 0, 1 << 20) % (room + 1)
    sizes = sizes.at[1:1 + 2 * twos:2].set(source_of - shifted).at[2:2 + 2 * twos:2].set(receiver + shifted)
    return sizes[jax.random.permutation(jax.random.fold_in(key, 2), count)]


def centred(key, extent, deviation, limit, split=(), held_as=jnp.bfloat16):
    factor_of = block_levels(key, extent, split, -0.22, 0.18) if split else 1.0
    values = jax.random.normal(key, extent, jnp.float32) * deviation * factor_of
    return jnp.minimum(jnp.maximum(values, -limit), limit).astype(held_as)


def setup_inputs(seed: int = 0) -> dict:
    seeds = jax.random.split(jax.random.key(seed), 7)
    return {
        "latent": centred(seeds[0], (FRAMES, ROW_CAP * N_TILE, LAT_COLS, CHANNELS), 1.0, 6.0, ((0, 4), (1, 8))),
        "tile_rows": uneven(seeds[1], N_TILE, TOTAL_ROWS, ROW_CAP, 2).astype(jnp.int32),
        "kernel_one": centred(seeds[2], (3, 3, 3, CHANNELS, CHANNELS), (27 * CHANNELS) ** -0.5, 0.078125),
        "bias_one": centred(seeds[3], (CHANNELS,), 0.5, 3.0, (), jnp.float32),
        "kernel_two": centred(seeds[4], (3, 3, 3, CHANNELS, CHANNELS), (27 * CHANNELS) ** -0.5, 0.078125),
        "bias_two": centred(seeds[5], (CHANNELS,), 0.5, 3.0, (), jnp.float32),
    }


def convolve(field, kernel, bias):
    padded = jnp.concatenate([field[0:1], field[0:1], field], axis=0)
    padded = jnp.pad(padded, ((0, 0), (1, 1), (1, 1), (0, 0)))
    result = lax.conv_general_dilated(padded[None], kernel.astype(jnp.float32), (1, 1, 1), "VALID",
                                      dimension_numbers=("NDHWC", "DHWIO", "NDHWC"),
                                      precision=lax.Precision.HIGHEST)
    return result[0] + bias.astype(jnp.float32)


def reference(latent, tile_rows, kernel_one, bias_one, kernel_two, bias_two):
    lengths = tile_rows.astype(jnp.int32)
    starts = (jnp.cumsum(lengths) - lengths).astype(jnp.int32)
    rows_global = jnp.arange(TOTAL_ROWS, dtype=jnp.int32)
    owner = (jnp.sum((starts[None, :] <= rows_global[:, None]).astype(jnp.int32), axis=1) - 1).astype(jnp.int32)
    source = (owner * ROW_CAP + rows_global - jnp.take(starts, owner)).astype(jnp.int32)
    image = jnp.take(latent, source, axis=1)
    upsampled = jnp.repeat(jnp.repeat(image, 2, axis=1), 2, axis=2).astype(jnp.float32)
    hidden = jax.nn.silu(convolve(upsampled, kernel_one, bias_one)).astype(jnp.bfloat16)
    mixed = (convolve(hidden.astype(jnp.float32), kernel_two, bias_two) + upsampled).astype(jnp.bfloat16)
    slots = jnp.arange(2 * ROW_CAP * N_TILE, dtype=jnp.int32)
    owner_slot = (slots // (2 * ROW_CAP)).astype(jnp.int32)
    offset = (slots % (2 * ROW_CAP)).astype(jnp.int32)
    valid = offset < 2 * jnp.take(lengths, owner_slot)
    target = jnp.clip(2 * jnp.take(starts, owner_slot) + offset, 0, 2 * TOTAL_ROWS - 1).astype(jnp.int32)
    placed = jnp.take(mixed, target, axis=1)
    return jnp.where(valid[None, :, None, None], placed, jnp.zeros((), jnp.bfloat16))
```

```python
import functools

import jax
import jax.numpy as jnp
from jax import lax
from jax.experimental import pallas as pl
from jax.experimental.pallas import tpu as pltpu
from jax.sharding import PartitionSpec as P

F32 = jnp.float32
BF16 = jnp.bfloat16
AXES = ("tm", "tile")
FIRST_STEP = 2
SECOND_STEP = 4


def rotated(block, axis):
    count = lax.axis_size(axis)
    return lax.ppermute(block, axis, [(i, (i + 1) % count) for i in range(count)])


def routes(groups, tiles, step, side):
    pairs = []
    for g in range(groups):
        for t in range(tiles):
            if side == "chip":
                to = t ^ 1
            else:
                to = t + 1 if t % 2 else t - 1
            if 0 <= to < tiles:
                pairs.append((g * tiles + t, ((g + step) % groups) * tiles + to))
            elif step:
                pairs.append((g * tiles + t, ((g + step) % groups) * tiles + t))
            else:
                pairs.append((g * tiles + t, (g ^ 1) * tiles + t))
    return pairs


def down(v):
    n = v.shape[-2]
    ids = lax.broadcasted_iota(jnp.int32, v.shape, v.ndim - 2)
    return jnp.where(ids == 0, 0.0, pltpu.roll(v, 1, v.ndim - 2))


def up(v):
    n = v.shape[-2]
    ids = lax.broadcasted_iota(jnp.int32, v.shape, v.ndim - 2)
    return jnp.where(ids == n - 1, 0.0, pltpu.roll(v, n - 1, v.ndim - 2))


def fold_kernel(k1_hbm, w1_ref, k1_ref, sem):
    chunk = 32
    cin = k1_ref.shape[3]
    copies = [pltpu.make_async_copy(k1_hbm.at[a], k1_ref.at[a], sem.at[a]) for a in range(3)]
    for copy in copies:
        copy.start()

    def pairs(x, y, z):
        return (x, y + z), (x + y, z)

    for a in range(3):
        copies[a].wait()

        def part(s, _):
            r0 = pl.multiple_of(s * chunk, chunk)
            rows = pl.ds(r0, chunk)
            g = [[k1_ref[a, p, q, rows, :].astype(F32) for q in range(3)] for p in range(3)]
            by_row = [pairs(g[0][q], g[1][q], g[2][q]) for q in range(3)]
            for r in range(2):
                for i in range(2):
                    taps = pairs(by_row[0][r][i], by_row[1][r][i], by_row[2][r][i])
                    for c in range(2):
                        for j in range(2):
                            w1_ref[r, c, a, i, j, rows, :] = taps[c][j].astype(BF16)
            return 0

        lax.fori_loop(0, cin // chunk, part, 0)


def main_kernel(
    rows_ref, b1_ref, b2_ref, x_ref, prev_ref, cross_ref, chip_ref, dcross_ref, dchip_ref,
    w1_ref, w2_ref, out_ref, xs, hs, mix
):
    frames, cap, cols, ch = x_ref.shape
    tiles = lax.axis_size("tile")
    group = lax.axis_index("tm")
    tile = lax.axis_index("tile")
    length = rows_ref[tile]
    odd = lax.rem(tile, 2) == 1
    half = cap + 1
    hid = frames + 2
    mid = slice(ch, 2 * ch)

    zero = jnp.zeros((frames, cols, ch), BF16)
    has_cross = jnp.logical_and(tile > 0, tile < tiles - 1)
    for base, own, cr, ci in ((frames, x_ref, cross_ref, chip_ref), (0, prev_ref, dcross_ref, dchip_ref)):
        cross = jnp.where(has_cross, cr[:, 0], zero)
        chip = ci[:, 0]
        xs[base:base + frames, 1:cap + 1, :, mid] = own[...]
        xs[base:base + frames, 0, :, mid] = jnp.where(odd, chip, cross)
        xs[base:base + frames, cap + 1, :, mid] = zero
        xs[base:base + frames, length + 1, :, mid] = jnp.where(odd, cross, chip)

    def neighbours(f, _):
        z = xs[f, :, :, mid].astype(F32)
        xs[f, :, :, 0:ch] = down(z).astype(BF16)
        xs[f, :, :, 2 * ch:3 * ch] = up(z).astype(BF16)
        return 0

    lax.fori_loop(0, 2 * frames, neighbours, 0)

    @pl.when(group == 0)
    def _():
        first = xs[frames]
        for f in range(frames):
            xs[f] = first

    bias_one = b1_ref[...]
    top = tile == 0
    bottom = tile == tiles - 1

    def dot(lhs, rhs):
        return jnp.dot(lhs, rhs, preferred_element_type=F32)

    def first_conv(f, n):
        for phase in range(2):
            act = []
            for c in range(2):
                lhs = jnp.concatenate(
                    [
                        xs[pl.ds(f + a, n), i:i + half, :, c * ch:(c + 2) * ch].reshape(n * half * cols, 2 * ch)
                        for a in range(3) for i in range(2)
                    ],
                    axis=1,
                )
                v = dot(lhs, w1_ref[phase, c].reshape(12 * ch, ch)) + bias_one
                v = v / (1.0 + jnp.exp(-v))
                act.append(v.reshape(n, half, cols, ch))
            he, ho = act
            k = lax.broadcasted_iota(jnp.int32, he.shape, 1)
            if phase == 0:
                keep = jnp.logical_not(jnp.logical_and(bottom, k == length))
            else:
                keep = jnp.logical_not(jnp.logical_and(top, k == 0))
            he = jnp.where(keep, he, 0.0)
            ho = jnp.where(keep, ho, 0.0)
            for c, value in enumerate((down(ho), he, ho, up(he))):
                hs[phase, pl.ds(f, n), :, :, c * ch:(c + 1) * ch] = value.astype(BF16)

    for f in range(0, hid, FIRST_STEP):
        first_conv(f, FIRST_STEP)

    bias_two = b2_ref[...]

    def second_conv(f, n):
        for r in range(2):
            rows = ((1, 0), (0, 0), (1, 1)) if r == 0 else ((0, 0), (1, 1), (0, 1))
            sums = []
            for c in range(2):
                lhs = jnp.concatenate(
                    [
                        hs[phase, pl.ds(f + a, n), k:k + cap, :, c * ch:(c + 3) * ch].reshape(n * cap * cols, 3 * ch)
                        for a in range(3) for phase, k in rows
                    ],
                    axis=1,
                )
                v = dot(lhs, w2_ref[...].reshape(27 * ch, ch)) + bias_two
                sums.append(v.reshape(n, cap, cols, ch))
            for g in range(n):
                for i in range(cap):
                    residual = xs[frames + f + g, i + 1, :, mid].astype(F32)
                    keep = i < length
                    for c in range(2):
                        value = jnp.where(keep, sums[c][g, i] + residual, 0.0)
                        for part in range(ch // 128):
                            mix[r, g, i, part, pl.ds(c, cols, stride=2), :] = value[:, 128 * part:128 * (part + 1)]
                    for part in range(ch // 128):
                        lanes = slice(128 * part, 128 * (part + 1))
                        out_ref[f + g, 2 * i + r, :, lanes] = mix[r, g, i, part].astype(BF16)

    for f in range(0, frames, SECOND_STEP):
        second_conv(f, SECOND_STEP)


def local(latent, tile_rows, kernel_one, bias_one, kernel_two, bias_two):
    frames, cap, cols, ch = latent.shape
    groups, tiles = lax.axis_size("tm"), lax.axis_size("tile")
    tile = lax.axis_index("tile")
    last = lax.dynamic_slice_in_dim(tile_rows, tile, 1)[0] - 1
    odd = lax.rem(tile, 2) == 1
    to_cross = lax.dynamic_slice_in_dim(latent, jnp.where(odd, last, 0), 1, axis=1)
    to_chip = lax.dynamic_slice_in_dim(latent, jnp.where(odd, 0, last), 1, axis=1)
    prev = rotated(latent, "tm")
    cross = lax.ppermute(to_cross, AXES, routes(groups, tiles, 0, "cross"))
    dcross = lax.ppermute(to_cross, AXES, routes(groups, tiles, 1, "cross"))
    dchip = lax.ppermute(to_chip, AXES, routes(groups, tiles, 1, "chip"))
    chip = lax.ppermute(to_chip, AXES, routes(groups, tiles, 0, "chip"))

    vmem = pl.BlockSpec(memory_space=pltpu.VMEM)
    smem = pl.BlockSpec(memory_space=pltpu.SMEM)
    w1 = pl.pallas_call(
        fold_kernel,
        out_shape=pltpu.VMEM((2, 2, 3, 2, 2, ch, ch), BF16),
        in_specs=[pl.BlockSpec(memory_space=pl.ANY)],
        out_specs=vmem,
        scratch_shapes=[pltpu.VMEM(kernel_one.shape, BF16), pltpu.SemaphoreType.DMA((3,))],
        compiler_params=pltpu.CompilerParams(vmem_limit_bytes=16 << 20),
        cost_estimate=pl.CostEstimate(flops=0, bytes_accessed=10 << 20, transcendentals=0),
        name="fold",
    )(kernel_one)
    w1 = pltpu.with_memory_space_constraint(w1, pltpu.VMEM)
    w2 = pltpu.with_memory_space_constraint(kernel_two, pltpu.VMEM)

    hid, ext = frames + 2, cap + 2
    return pl.pallas_call(
        main_kernel,
        out_shape=jax.ShapeDtypeStruct((frames, 2 * cap, 2 * cols, ch), BF16),
        in_specs=[smem] + [vmem] * 10,
        out_specs=vmem,
        scratch_shapes=[
            pltpu.VMEM((2 * frames, ext, cols, 3 * ch), BF16),
            pltpu.VMEM((2, hid, cap + 1, cols, 4 * ch), BF16),
            pltpu.VMEM((2, SECOND_STEP, cap, ch // 128, 2 * cols, 128), F32),
        ],
        compiler_params=pltpu.CompilerParams(vmem_limit_bytes=36 << 20),
        cost_estimate=pl.CostEstimate(flops=13 << 30, bytes_accessed=2 << 20, transcendentals=0),
        name="decode",
    )(tile_rows, bias_one.reshape(1, ch), bias_two.reshape(1, ch), latent, prev, cross, chip, dcross, dchip, w1, w2)


def solution(mesh):
    in_specs = (P("tm", "tile", None, None), P(), P(), P(), P(), P())
    out_specs = P("tm", "tile", None, None)
    return jax.shard_map(local, mesh=mesh, in_specs=in_specs, out_specs=out_specs, check_vma=False)
```

```python
import functools

import jax
import jax.numpy as jnp
from jax import lax
from jax.experimental import pallas as pl
from jax.experimental.pallas import tpu as pltpu
from jax.sharding import PartitionSpec as P

F32 = jnp.float32
BF16 = jnp.bfloat16
AXES = ("tm", "tile")
FIRST_STEP = 2


def rotated(block, axis):
    count = lax.axis_size(axis)
    return lax.ppermute(block, axis, [(i, (i + 1) % count) for i in range(count)])


def routes(groups, tiles, step, side):
    pairs = []
    for g in range(groups):
        for t in range(tiles):
            if side == "chip":
                to = t ^ 1
            else:
                to = t + 1 if t % 2 else t - 1
            if 0 <= to < tiles:
                pairs.append((g * tiles + t, ((g + step) % groups) * tiles + to))
            elif step:
                pairs.append((g * tiles + t, ((g + step) % groups) * tiles + t))
            else:
                pairs.append((g * tiles + t, g * tiles + tiles - 1 - t))
    return pairs


def down(v):
    n = v.shape[-2]
    ids = lax.broadcasted_iota(jnp.int32, v.shape, v.ndim - 2)
    return jnp.where(ids == 0, 0.0, pltpu.roll(v, 1, v.ndim - 2))


def up(v):
    n = v.shape[-2]
    ids = lax.broadcasted_iota(jnp.int32, v.shape, v.ndim - 2)
    return jnp.where(ids == n - 1, 0.0, pltpu.roll(v, n - 1, v.ndim - 2))


def pick_kernel(rows_hbm, x_hbm, cross_ref, chip_ref, rows_ref, x_ref, sem):
    copies = [
        pltpu.make_async_copy(rows_hbm, rows_ref, sem.at[0]),
        pltpu.make_async_copy(x_hbm, x_ref, sem.at[1]),
    ]
    for copy in copies:
        copy.start()
    for copy in copies:
        copy.wait()
    tile = lax.axis_index("tile")
    last = rows_ref[tile] - 1
    odd = lax.rem(tile, 2) == 1
    cross_ref[:, 0] = x_ref[:, jnp.where(odd, last, 0)]
    chip_ref[:, 0] = x_ref[:, jnp.where(odd, 0, last)]


def assemble(xs, own, cross_ref, chip_ref, chip_row, length):
    frames, cap, cols, ch = own.shape
    tile = lax.axis_index("tile")
    odd = lax.rem(tile, 2) == 1
    mid = slice(ch, 2 * ch)
    zero = jnp.zeros((frames, cols, ch), BF16)
    has_cross = jnp.logical_and(tile > 0, tile < lax.axis_size("tile") - 1)
    cross = jnp.where(has_cross, cross_ref[:, 0], zero)
    chip = chip_ref[:, chip_row]
    xs[:, 1:cap + 1, :, mid] = own[...]
    xs[:, 0, :, mid] = jnp.where(odd, chip, cross)
    xs[:, cap + 1, :, mid] = zero
    xs[:, length + 1, :, mid] = jnp.where(odd, cross, chip)

    def neighbours(f, _):
        z = xs[f, :, :, mid].astype(F32)
        xs[f, :, :, 0:ch] = down(z).astype(BF16)
        xs[f, :, :, 2 * ch:3 * ch] = up(z).astype(BF16)
        return 0

    lax.fori_loop(0, frames, neighbours, 0)


def dot(lhs, rhs):
    return jnp.dot(lhs, rhs, preferred_element_type=F32)


def first_conv(sources, w1_ref, bias, hs, f, length):
    n = len(sources)
    _, _, half, cols, wide = hs.shape
    ch = wide // 4
    tile = lax.axis_index("tile")
    top = tile == 0
    bottom = tile == lax.axis_size("tile") - 1
    for phase in range(2):
        act = []
        for c in range(2):
            lhs = jnp.concatenate(
                [
                    jnp.concatenate(
                        [
                            ref[g, i:i + half, :, c * ch:(c + 2) * ch].reshape(half * cols, 2 * ch)
                            for a in range(3) for i in range(2) for ref, g in [taps[a]]
                        ],
                        axis=1,
                    )
                    for taps in sources
                ],
                axis=0,
            )
            v = dot(lhs, w1_ref[phase, c].reshape(12 * ch, ch)) + bias
            v = v / (1.0 + jnp.exp(-v))
            act.append(v.reshape(n, half, cols, ch))
        he, ho = act
        k = lax.broadcasted_iota(jnp.int32, he.shape, 1)
        if phase == 0:
            keep = jnp.logical_not(jnp.logical_and(bottom, k == length))
        else:
            keep = jnp.logical_not(jnp.logical_and(top, k == 0))
        he = jnp.where(keep, he, 0.0)
        ho = jnp.where(keep, ho, 0.0)
        for c, value in enumerate((down(ho) - ho, he + ho, ho - he, he - up(he))):
            hs[phase, f:f + n, :, :, c * ch:(c + 1) * ch] = value.astype(BF16)


def fold_kernel(k1_hbm, k2_hbm, w1_ref, w2_ref, k1_ref, k2_ref, sem):
    chunk = 32
    cin = k1_ref.shape[3]
    copies = [
        pltpu.make_async_copy(source.at[a], target.at[a], sem.at[3 * n + a])
        for n, (source, target) in enumerate(((k1_hbm, k1_ref), (k2_hbm, k2_ref))) for a in range(3)
    ]
    for copy in copies:
        copy.start()

    def pairs(x, y, z):
        return (x, y + z), (x + y, z)

    for a in range(3):
        copies[a].wait()

        def part(s, _):
            r0 = pl.multiple_of(s * chunk, chunk)
            rows = pl.ds(r0, chunk)
            g = [[k1_ref[a, p, q, rows, :].astype(F32) for q in range(3)] for p in range(3)]
            by_row = [pairs(g[0][q], g[1][q], g[2][q]) for q in range(3)]
            for r in range(2):
                for i in range(2):
                    taps = pairs(by_row[0][r][i], by_row[1][r][i], by_row[2][r][i])
                    for c in range(2):
                        for j in range(2):
                            w1_ref[r, c, a, i, j, rows, :] = taps[c][j].astype(BF16)
            return 0

        lax.fori_loop(0, cin // chunk, part, 0)

    for a in range(3):
        copies[3 + a].wait()

        def spread(s, _):
            r0 = pl.multiple_of(s * chunk, chunk)
            rows = pl.ds(r0, chunk)
            for p in range(3):
                x, y, z = (k2_ref[a, p, q, rows, :] for q in range(3))
                even = (x.astype(F32) + z.astype(F32)) * 0.5
                odd = y.astype(F32) * 0.5
                w2_ref[0, a, p, rows, :] = x
                w2_ref[1, a, p, rows, :] = (even + odd).astype(BF16)
                w2_ref[2, a, p, rows, :] = (even - odd).astype(BF16)
                w2_ref[3, a, p, rows, :] = z
            return 0

        lax.fori_loop(0, cin // chunk, spread, 0)


def own_kernel(rows_ref, b1_ref, x_ref, cross_ref, chip_ref, w1_ref, xs, hs):
    frames = x_ref.shape[0]
    length = rows_ref[lax.axis_index("tile")]
    assemble(xs, x_ref, cross_ref, chip_ref, 0, length)
    own = hs.shape[1]
    sources = [[(xs, frames - 2 - own + n + a) for a in range(3)] for n in range(own)]
    first_conv(sources, w1_ref, b1_ref[...], hs, 0, length)


def rest_kernel(
    rows_ref, b1_ref, b2_ref, prev_ref, dcross_ref, dchip_ref, xo, ho, w1_ref, w2_ref, out_ref, xp, hp, mix
):
    frames, cap, cols, ch = prev_ref.shape
    tile = lax.axis_index("tile")
    length = rows_ref[tile]
    assemble(xp, prev_ref, dcross_ref, dchip_ref, 0, length)

    @pl.when(lax.axis_index("tm") == 0)
    def _():
        first = xo[0]
        for f in range(frames):
            xp[f] = first

    shared = hp.shape[1]
    source = [(xp, f) for f in range(frames)] + [(xo, f) for f in range(frames)]
    for f in range(0, shared, FIRST_STEP):
        first_conv(
            [[source[f + n + a] for a in range(3)] for n in range(FIRST_STEP)], w1_ref, b1_ref[...], hp, f, length
        )

    bias_two = b2_ref[...]
    hidden = [(hp, f) for f in range(shared)] + [(ho, f) for f in range(ho.shape[1])]
    for r in range(2):
        rows = ((1, 0), (0, 0), (1, 1)) if r == 0 else ((0, 0), (1, 1), (0, 1))
        m = []
        for c in range(4):
            lhs = jnp.concatenate(
                [
                    jnp.concatenate(
                        [
                            ref[phase, g, k:k + cap, :, c * ch:(c + 1) * ch].reshape(cap * cols, ch)
                            for a in range(3) for phase, k in rows for ref, g in [hidden[f + a]]
                        ],
                        axis=1,
                    )
                    for f in range(frames)
                ],
                axis=0,
            )
            m.append(dot(lhs, w2_ref[c].reshape(9 * ch, ch)))
        sums = [
            (v + bias_two).reshape(frames, cap, cols, ch) for v in (m[0] + (m[1] + m[2]), (m[1] - m[2]) - m[3])
        ]
        for f in range(frames):
            for i in range(cap):
                residual = xo[f, i + 1, :, ch:2 * ch].astype(F32)
                keep = i < length
                for c in range(2):
                    value = jnp.where(keep, sums[c][f, i] + residual, 0.0)
                    for part in range(ch // 128):
                        mix[r, f, i, part, pl.ds(c, cols, stride=2), :] = value[:, 128 * part:128 * (part + 1)]
                for part in range(ch // 128):
                    lanes = slice(128 * part, 128 * (part + 1))
                    out_ref[f, 2 * i + r, :, lanes] = mix[r, f, i, part].astype(BF16)


def in_hbm(value):
    return pltpu.with_memory_space_constraint(value, pltpu.HBM)


def in_vmem(value):
    return pltpu.with_memory_space_constraint(value, pltpu.VMEM)


def local(latent, tile_rows, kernel_one, bias_one, kernel_two, bias_two):
    frames, cap, cols, ch = latent.shape
    groups, tiles = lax.axis_size("tm"), lax.axis_size("tile")
    vmem = pl.BlockSpec(memory_space=pltpu.VMEM)
    smem = pl.BlockSpec(memory_space=pltpu.SMEM)
    hbm = pl.BlockSpec(memory_space=pltpu.HBM)
    bias_one, bias_two = bias_one.reshape(1, ch), bias_two.reshape(1, ch)

    prev = rotated(latent, "tm")
    rim = pltpu.VMEM((frames, 1, cols, ch), BF16)
    to_cross, to_chip = pl.pallas_call(
        pick_kernel,
        out_shape=(rim, rim),
        in_specs=[hbm, hbm],
        out_specs=(vmem, vmem),
        scratch_shapes=[
            pltpu.SMEM(tile_rows.shape, jnp.int32),
            pltpu.VMEM(latent.shape, BF16),
            pltpu.SemaphoreType.DMA((2,)),
        ],
        compiler_params=pltpu.CompilerParams(vmem_limit_bytes=4 << 20),
        cost_estimate=pl.CostEstimate(flops=0, bytes_accessed=1 << 19, transcendentals=0),
        name="pick",
    )(in_hbm(tile_rows), in_hbm(latent))
    chip = lax.ppermute(to_chip, AXES, routes(groups, tiles, 0, "chip"))
    cross = lax.ppermute(to_cross, AXES, routes(groups, tiles, 0, "cross"))
    dcross = lax.ppermute(to_cross, AXES, routes(groups, tiles, 1, "cross"))
    dchip = lax.ppermute(to_chip, AXES, routes(groups, tiles, 1, "chip"))

    w1, w2 = pl.pallas_call(
        fold_kernel,
        out_shape=(pltpu.VMEM((2, 2, 3, 2, 2, ch, ch), BF16), pltpu.VMEM((4, 3, 3, ch, ch), BF16)),
        in_specs=[hbm, hbm],
        out_specs=(vmem, vmem),
        scratch_shapes=[
            pltpu.VMEM(kernel_one.shape, BF16),
            pltpu.VMEM(kernel_two.shape, BF16),
            pltpu.SemaphoreType.DMA((6,)),
        ],
        compiler_params=pltpu.CompilerParams(vmem_limit_bytes=16 << 20),
        cost_estimate=pl.CostEstimate(flops=0, bytes_accessed=8 << 20, transcendentals=0),
        name="fold",
    )(in_hbm(kernel_one), in_hbm(kernel_two))
    w1, w2 = in_vmem(w1), in_vmem(w2)

    own = frames - 2
    xo, ho = pl.pallas_call(
        own_kernel,
        out_shape=(
            pltpu.VMEM((frames, cap + 2, cols, 3 * ch), BF16),
            pltpu.VMEM((2, own, cap + 1, cols, 4 * ch), BF16),
        ),
        in_specs=[smem] + [vmem] * 5,
        out_specs=(vmem, vmem),
        compiler_params=pltpu.CompilerParams(vmem_limit_bytes=24 << 20),
        cost_estimate=pl.CostEstimate(flops=0, bytes_accessed=8 << 20, transcendentals=0),
        name="own",
    )(tile_rows, bias_one, latent, cross, chip, w1)

    return pl.pallas_call(
        rest_kernel,
        out_shape=jax.ShapeDtypeStruct((frames, 2 * cap, 2 * cols, ch), BF16),
        in_specs=[smem] + [vmem] * 9,
        out_specs=vmem,
        scratch_shapes=[
            pltpu.VMEM((frames, cap + 2, cols, 3 * ch), BF16),
            pltpu.VMEM((2, frames, cap + 1, cols, 4 * ch), BF16),
            pltpu.VMEM((2, frames, cap, ch // 128, 2 * cols, 128), F32),
        ],
        compiler_params=pltpu.CompilerParams(vmem_limit_bytes=36 << 20),
        cost_estimate=pl.CostEstimate(flops=10 << 30, bytes_accessed=2 << 20, transcendentals=0),
        name="rest",
    )(
        tile_rows, bias_one, bias_two, prev, dcross, dchip,
        in_vmem(xo), in_vmem(ho), w1, w2,
    )


def solution(mesh):
    in_specs = (P("tm", "tile", None, None), P(), P(), P(), P(), P())
    out_specs = P("tm", "tile", None, None)
    return jax.shard_map(local, mesh=mesh, in_specs=in_specs, out_specs=out_specs, check_vma=False)
```

```python
import functools

import jax
import jax.numpy as jnp
from jax import lax
from jax.experimental import pallas as pl
from jax.experimental.pallas import tpu as pltpu
from jax.sharding import PartitionSpec as P

F32 = jnp.float32
BF16 = jnp.bfloat16
AXES = ("tm", "tile")
FIRST_STEP = 2
CHUNK = 32


def rotated(block, axis):
    count = lax.axis_size(axis)
    return lax.ppermute(block, axis, [(i, (i + 1) % count) for i in range(count)])


def routes(groups, tiles, step, side):
    pairs = []
    for g in range(groups):
        for t in range(tiles):
            if side == "chip":
                to = t ^ 1
            else:
                to = t + 1 if t % 2 else t - 1
            if 0 <= to < tiles:
                pairs.append((g * tiles + t, ((g + step) % groups) * tiles + to))
            elif step:
                pairs.append((g * tiles + t, ((g + step) % groups) * tiles + t))
            else:
                pairs.append((g * tiles + t, g * tiles + tiles - 1 - t))
    return pairs


def down(v):
    n = v.shape[-2]
    ids = lax.broadcasted_iota(jnp.int32, v.shape, v.ndim - 2)
    return jnp.where(ids == 0, 0.0, pltpu.roll(v, 1, v.ndim - 2))


def up(v):
    n = v.shape[-2]
    ids = lax.broadcasted_iota(jnp.int32, v.shape, v.ndim - 2)
    return jnp.where(ids == n - 1, 0.0, pltpu.roll(v, n - 1, v.ndim - 2))


def pick_kernel(rows_hbm, x_hbm, _, __, cross_ref, chip_ref, rows_ref, x_ref, sem):
    copies = [
        pltpu.make_async_copy(rows_hbm, rows_ref, sem.at[0]),
        pltpu.make_async_copy(x_hbm, x_ref, sem.at[1]),
    ]
    for copy in copies:
        copy.start()
    for copy in copies:
        copy.wait()
    tile = lax.axis_index("tile")
    last = rows_ref[tile] - 1
    odd = lax.rem(tile, 2) == 1
    cross_ref[:, 0] = x_ref[:, jnp.where(odd, last, 0)]
    chip_ref[:, 0] = x_ref[:, jnp.where(odd, 0, last)]


def assemble(xs, own, cross_ref, chip_ref, chip_row, length, instead=None):
    frames, cap, cols, ch = own.shape
    tile = lax.axis_index("tile")
    odd = lax.rem(tile, 2) == 1
    has_cross = jnp.logical_and(tile > 0, tile < lax.axis_size("tile") - 1)
    for f in range(frames):
        cross = jnp.where(has_cross, cross_ref[f, 0], jnp.zeros((cols, ch), BF16))
        chip = chip_ref[f, chip_row]
        below = jnp.where(odd, cross, chip)
        rows = [jnp.where(odd, chip, cross), own[f, 0]]
        rows += [jnp.where(length == i, below, own[f, i]) for i in range(1, cap)] + [below]
        for i, z in enumerate(rows):
            if instead is not None:
                z = jnp.where(instead[0], instead[1][i], z)
            wide = z.astype(F32)
            xs[f, i, :, 0:ch] = down(wide).astype(BF16)
            xs[f, i, :, ch:2 * ch] = z
            xs[f, i, :, 2 * ch:3 * ch] = up(wide).astype(BF16)


def dot(lhs, rhs):
    return jnp.dot(lhs, rhs, preferred_element_type=F32)


def first_conv(sources, weights, bias, hs, f, length, beside):
    n = len(sources)
    _, _, half, cols, wide = hs.shape
    ch = wide // 4
    tile = lax.axis_index("tile")
    top = tile == 0
    bottom = tile == lax.axis_size("tile") - 1
    for phase in range(2):
        act = []
        for c in range(2):
            lhs = jnp.concatenate(
                [
                    jnp.concatenate(
                        [
                            ref[g, i:i + half, :, c * ch:(c + 2) * ch].reshape(half * cols, 2 * ch)
                            for a in range(3) for i in range(2) for ref, g in [taps[a]]
                        ],
                        axis=1,
                    )
                    for taps in sources
                ],
                axis=0,
            )
            v = dot(lhs, weights[phase][c].reshape(12 * ch, ch)) + bias
            for task in beside[2 * phase + c]:
                task()
            v = v / (1.0 + jnp.exp(-v))
            act.append(v.reshape(n, half, cols, ch))
        he, ho = act
        k = lax.broadcasted_iota(jnp.int32, he.shape, 1)
        if phase == 0:
            keep = jnp.logical_not(jnp.logical_and(bottom, k == length))
        else:
            keep = jnp.logical_not(jnp.logical_and(top, k == 0))
        he = jnp.where(keep, he, 0.0)
        ho = jnp.where(keep, ho, 0.0)
        for c, value in enumerate((down(ho) - ho, he + ho, ho - he, he - up(he))):
            hs[phase, f:f + n, :, :, c * ch:(c + 1) * ch] = value.astype(BF16)


def fold(k1_ref, w_ref, phase, a, rows):
    def pairs(x, y, z):
        return (x, y + z), (x + y, z)

    g = [[k1_ref[a, p, q, rows].astype(F32) for q in range(3)] for p in range(3)]
    by_row = [pairs(g[0][q], g[1][q], g[2][q])[phase] for q in range(3)]
    for i in range(2):
        taps = pairs(by_row[0][i], by_row[1][i], by_row[2][i])
        for c in range(2):
            for j in range(2):
                if i == phase and c == j:
                    w_ref[c, a, i, j, rows] = k1_ref[a, 2 * i, 2 * j, rows]
                else:
                    w_ref[c, a, i, j, rows] = taps[c][j].astype(BF16)


def fold_kernel(k1_ref, w_ref):
    parts = k1_ref.shape[3] // CHUNK

    def part(s, _):
        fold(k1_ref, w_ref, 0, s // parts, pl.ds(pl.multiple_of(lax.rem(s, parts) * CHUNK, CHUNK), CHUNK))
        return 0

    lax.fori_loop(0, 3 * parts, part, 0)


def spread(k2_ref, w2_ref, a, p, rows):
    x, y, z = (k2_ref[a, p, q, rows].astype(F32) * 0.5 for q in range(3))
    even = x + z
    w2_ref[0, a, p, rows] = (even + y).astype(BF16)
    w2_ref[1, a, p, rows] = (even - y).astype(BF16)


def own_kernel(rows_ref, b1_ref, x_ref, cross_ref, chip_ref, k1_ref, wa_ref, xs, hs, wb_ref):
    frames = x_ref.shape[0]
    length = rows_ref[lax.axis_index("tile")]
    assemble(xs, x_ref, cross_ref, chip_ref, 0, length)
    own = hs.shape[1]
    sources = [[(xs, frames - 2 - own + n + a) for a in range(3)] for n in range(own)]
    tasks = [
        functools.partial(fold, k1_ref, wb_ref, 1, a, slice(r, r + CHUNK))
        for a in range(3) for r in range(0, k1_ref.shape[3], CHUNK)
    ]
    first_conv(
        sources, (wa_ref, wb_ref), b1_ref[...], hs, 0, length, (tasks[0::2], tasks[1::2], (), ())
    )


def rest_kernel(
    rows_ref, b1_ref, b2_ref, prev_ref, dcross_ref, dchip_ref, xo, ho, wa_ref, wb_ref, k2_ref, out_hbm, xp, hp, w2_ref, mix, stage, sem
):
    frames, cap, cols, ch = prev_ref.shape
    tile = lax.axis_index("tile")
    length = rows_ref[tile]
    first = [xo[0, i, :, ch:2 * ch] for i in range(cap + 2)]
    assemble(xp, prev_ref, dcross_ref, dchip_ref, 0, length, (lax.axis_index("tm") == 0, first))

    tasks = [
        functools.partial(spread, k2_ref, w2_ref, a, p, slice(r, r + CHUNK))
        for a in range(3) for p in range(3) for r in range(0, k2_ref.shape[3], CHUNK)
    ]
    shared = hp.shape[1]
    source = [(xp, f) for f in range(frames)] + [(xo, f) for f in range(frames)]
    for f in range(0, shared, FIRST_STEP):
        first_conv(
            [[source[f + n + a] for a in range(3)] for n in range(FIRST_STEP)], (wa_ref, wb_ref), b1_ref[...], hp, f,
            length, [tasks[n::2 * shared] for n in range(2 * f, 2 * f + 4)],
        )

    bias_two = b2_ref[...]
    copies = []
    hidden = [(hp, f) for f in range(shared)] + [(ho, f) for f in range(ho.shape[1])]
    for r in range(2):
        rows = ((1, 0), (0, 0), (1, 1)) if r == 0 else ((0, 0), (1, 1), (0, 1))
        m = []
        for c in range(4):
            lhs = jnp.concatenate(
                [
                    jnp.concatenate(
                        [
                            ref[phase, g, k:k + cap, :, c * ch:(c + 1) * ch].reshape(cap * cols, ch)
                            for a in range(3) for phase, k in rows for ref, g in [hidden[f + a]]
                        ],
                        axis=1,
                    )
                    for f in range(frames)
                ],
                axis=0,
            )
            if c in (1, 2):
                taps = w2_ref[c - 1].reshape(9 * ch, ch)
            else:
                taps = jnp.concatenate([k2_ref[a, p, 2 * (c // 3)] for a in range(3) for p in range(3)], axis=0)
            m.append(dot(lhs, taps))
        sums = [
            (v + bias_two).reshape(frames, cap, cols, ch) for v in (m[0] + (m[1] + m[2]), (m[1] - m[2]) - m[3])
        ]
        for f in range(frames):
            for i in range(cap):
                residual = xo[f, i + 1, :, ch:2 * ch].astype(F32)
                keep = i < length
                for c in range(2):
                    value = jnp.where(keep, sums[c][f, i] + residual, 0.0)
                    for part in range(ch // 128):
                        mix[r, f, i, part, pl.ds(c, cols, stride=2), :] = value[:, 128 * part:128 * (part + 1)]
                for part in range(ch // 128):
                    lanes = slice(128 * part, 128 * (part + 1))
                    stage[r, f, i, :, lanes] = mix[r, f, i, part].astype(BF16)
            copies.append(pltpu.make_async_copy(stage.at[r, f], out_hbm.at[f, :, r], sem.at[r, f]))
            copies[-1].start()
    for copy in copies:
        copy.wait()


def in_hbm(value):
    return pltpu.with_memory_space_constraint(value, pltpu.HBM)


def in_vmem(value):
    return pltpu.with_memory_space_constraint(value, pltpu.VMEM)


def local(latent, tile_rows, kernel_one, bias_one, kernel_two, bias_two):
    frames, cap, cols, ch = latent.shape
    groups, tiles = lax.axis_size("tm"), lax.axis_size("tile")
    vmem = pl.BlockSpec(memory_space=pltpu.VMEM)
    smem = pl.BlockSpec(memory_space=pltpu.SMEM)
    hbm = pl.BlockSpec(memory_space=pltpu.HBM)
    bias_one, bias_two = bias_one.reshape(1, ch), bias_two.reshape(1, ch)

    prev = rotated(latent, "tm")
    rim = pltpu.VMEM((frames, 1, cols, ch), BF16)
    to_cross, to_chip = pl.pallas_call(
        pick_kernel,
        out_shape=(rim, rim),
        in_specs=[hbm] * 4,
        out_specs=(vmem, vmem),
        scratch_shapes=[
            pltpu.SMEM(tile_rows.shape, jnp.int32),
            pltpu.VMEM(latent.shape, BF16),
            pltpu.SemaphoreType.DMA((2,)),
        ],
        compiler_params=pltpu.CompilerParams(vmem_limit_bytes=4 << 20),
        cost_estimate=pl.CostEstimate(flops=0, bytes_accessed=1 << 19, transcendentals=0),
        name="pick",
    )(in_hbm(tile_rows), in_hbm(latent), in_hbm(kernel_one), in_hbm(kernel_two))
    chip = lax.ppermute(to_chip, AXES, routes(groups, tiles, 0, "chip"))
    cross = lax.ppermute(to_cross, AXES, routes(groups, tiles, 0, "cross"))
    dcross = lax.ppermute(to_cross, AXES, routes(groups, tiles, 1, "cross"))
    dchip = lax.ppermute(to_chip, AXES, routes(groups, tiles, 1, "chip"))

    kernel_one, kernel_two = in_vmem(kernel_one), in_vmem(kernel_two)
    folded = pltpu.VMEM((2, 3, 2, 2, ch, ch), BF16)
    wa = pl.pallas_call(
        fold_kernel,
        out_shape=folded,
        in_specs=[vmem],
        out_specs=vmem,
        compiler_params=pltpu.CompilerParams(vmem_limit_bytes=4 << 20),
        cost_estimate=pl.CostEstimate(flops=0, bytes_accessed=8 << 20, transcendentals=0),
        name="fold",
    )(kernel_one)
    wa = in_vmem(wa)

    own = frames - 2
    xo, ho, wb = pl.pallas_call(
        own_kernel,
        out_shape=(
            pltpu.VMEM((frames, cap + 2, cols, 3 * ch), BF16),
            pltpu.VMEM((2, own, cap + 1, cols, 4 * ch), BF16),
            folded,
        ),
        in_specs=[smem] + [vmem] * 6,
        out_specs=(vmem, vmem, vmem),
        compiler_params=pltpu.CompilerParams(vmem_limit_bytes=20 << 20),
        cost_estimate=pl.CostEstimate(flops=0, bytes_accessed=8 << 20, transcendentals=0),
        name="own",
    )(tile_rows, bias_one, latent, cross, chip, kernel_one, wa)

    mixed = pl.pallas_call(
        rest_kernel,
        out_shape=jax.ShapeDtypeStruct((frames, cap, 2, 2 * cols, ch), BF16),
        in_specs=[smem] + [vmem] * 10,
        out_specs=hbm,
        scratch_shapes=[
            pltpu.VMEM((frames, cap + 2, cols, 3 * ch), BF16),
            pltpu.VMEM((2, frames, cap + 1, cols, 4 * ch), BF16),
            pltpu.VMEM((2, 3, 3, ch, ch), BF16),
            pltpu.VMEM((2, frames, cap, ch // 128, 2 * cols, 128), F32),
            pltpu.VMEM((2, frames, cap, 2 * cols, ch), BF16),
            pltpu.SemaphoreType.DMA((2, frames)),
        ],
        compiler_params=pltpu.CompilerParams(vmem_limit_bytes=36 << 20),
        cost_estimate=pl.CostEstimate(flops=10 << 30, bytes_accessed=2 << 20, transcendentals=0),
        name="rest",
    )(
        tile_rows, bias_one, bias_two, prev, dcross, dchip,
        in_vmem(xo), in_vmem(ho), wa, in_vmem(wb), kernel_two,
    )
    return mixed.reshape(frames, 2 * cap, 2 * cols, ch)


def solution(mesh):
    in_specs = (P("tm", "tile", None, None), P(), P(), P(), P(), P())
    out_specs = P("tm", "tile", None, None)
    return jax.shard_map(local, mesh=mesh, in_specs=in_specs, out_specs=out_specs, check_vma=False)
```

```python
import functools

import jax
import jax.numpy as jnp
from jax import lax
from jax.experimental import pallas as pl
from jax.experimental.pallas import tpu as pltpu
from jax.sharding import PartitionSpec as P

F32 = jnp.float32
BF16 = jnp.bfloat16
AXES = ("tm", "tile")
FIRST_STEP = 2
CHUNK = 32


def rotated(block, axis):
    count = lax.axis_size(axis)
    return lax.ppermute(block, axis, [(i, (i + 1) % count) for i in range(count)])


def routes(groups, tiles, step, side):
    pairs = []
    for g in range(groups):
        for t in range(tiles):
            if side == "chip":
                to = t ^ 1
            else:
                to = t + 1 if t % 2 else t - 1
            if 0 <= to < tiles:
                pairs.append((g * tiles + t, ((g + step) % groups) * tiles + to))
            else:
                pairs.append((g * tiles + t, g * tiles + tiles - 1 - t))
    return pairs


def down(v):
    n = v.shape[-2]
    ids = lax.broadcasted_iota(jnp.int32, v.shape, v.ndim - 2)
    return jnp.where(ids == 0, 0.0, pltpu.roll(v, 1, v.ndim - 2))


def up(v):
    n = v.shape[-2]
    ids = lax.broadcasted_iota(jnp.int32, v.shape, v.ndim - 2)
    return jnp.where(ids == n - 1, 0.0, pltpu.roll(v, n - 1, v.ndim - 2))


def pick_kernel(rows_hbm, x_hbm, _, __, cross_ref, chip_ref, rows_ref, x_ref, sem):
    copies = [
        pltpu.make_async_copy(rows_hbm, rows_ref, sem.at[0]),
        pltpu.make_async_copy(x_hbm, x_ref, sem.at[1]),
    ]
    for copy in copies:
        copy.start()
    for copy in copies:
        copy.wait()
    tile = lax.axis_index("tile")
    last = rows_ref[tile] - 1
    odd = lax.rem(tile, 2) == 1
    cross_ref[:, 0] = x_ref[:, jnp.where(odd, last, 0)]
    chip_ref[:, 0] = x_ref[:, jnp.where(odd, 0, last)]


def assemble(xs, own, cross_ref, chip_ref, chip_row, length, instead=None):
    frames, cap, cols, ch = own.shape
    tile = lax.axis_index("tile")
    odd = lax.rem(tile, 2) == 1
    has_cross = jnp.logical_and(tile > 0, tile < lax.axis_size("tile") - 1)
    for f in range(frames):
        cross = jnp.where(has_cross, cross_ref[f, 0], jnp.zeros((cols, ch), BF16))
        chip = chip_ref[f, chip_row]
        below = jnp.where(odd, cross, chip)
        rows = [jnp.where(odd, chip, cross), own[f, 0]]
        rows += [jnp.where(length == i, below, own[f, i]) for i in range(1, cap)] + [below]
        for i, z in enumerate(rows):
            if instead is not None:
                z = jnp.where(instead[0], instead[1][i], z)
            wide = z.astype(F32)
            xs[f, i, :, 0:ch] = down(wide).astype(BF16)
            xs[f, i, :, ch:2 * ch] = z
            xs[f, i, :, 2 * ch:3 * ch] = up(wide).astype(BF16)


def dot(lhs, rhs):
    return jnp.dot(lhs, rhs, preferred_element_type=F32)


def first_conv(sources, weights, bias, hs, f, length, beside):
    n = len(sources)
    _, _, half, cols, wide = hs.shape
    ch = wide // 4
    tile = lax.axis_index("tile")
    top = tile == 0
    bottom = tile == lax.axis_size("tile") - 1
    for phase in range(2):
        act = []
        for c in range(2):
            lhs = jnp.concatenate(
                [
                    jnp.concatenate(
                        [
                            ref[g, i:i + half, :, c * ch:(c + 2) * ch].reshape(half * cols, 2 * ch)
                            for a in range(3) for i in range(2) for ref, g in [taps[a]]
                        ],
                        axis=1,
                    )
                    for taps in sources
                ],
                axis=0,
            )
            v = dot(lhs, weights[phase][c].reshape(12 * ch, ch)) + bias
            for task in beside[2 * phase + c]:
                task()
            v = v / (1.0 + jnp.exp(-v))
            act.append(v.reshape(n, half, cols, ch))
        he, ho = act
        k = lax.broadcasted_iota(jnp.int32, he.shape, 1)
        if phase == 0:
            keep = jnp.logical_not(jnp.logical_and(bottom, k == length))
        else:
            keep = jnp.logical_not(jnp.logical_and(top, k == 0))
        he = jnp.where(keep, he, 0.0)
        ho = jnp.where(keep, ho, 0.0)
        for c, value in enumerate((down(ho) - ho, he + ho, ho - he, he - up(he))):
            hs[phase, f:f + n, :, :, c * ch:(c + 1) * ch] = value.astype(BF16)


def fold(k1_ref, w_ref, phase, a, rows):
    def pairs(x, y, z):
        return (x, y + z), (x + y, z)

    g = [[k1_ref[a, p, q, rows].astype(F32) for q in range(3)] for p in range(3)]
    by_row = [pairs(g[0][q], g[1][q], g[2][q])[phase] for q in range(3)]
    for i in range(2):
        taps = pairs(by_row[0][i], by_row[1][i], by_row[2][i])
        for c in range(2):
            for j in range(2):
                if i == phase and c == j:
                    w_ref[c, a, i, j, rows] = k1_ref[a, 2 * i, 2 * j, rows]
                else:
                    w_ref[c, a, i, j, rows] = taps[c][j].astype(BF16)


def fold_kernel(k1_ref, w_ref):
    parts = k1_ref.shape[3] // CHUNK

    def part(s, _):
        fold(k1_ref, w_ref, 0, s // parts, pl.ds(pl.multiple_of(lax.rem(s, parts) * CHUNK, CHUNK), CHUNK))
        return 0

    lax.fori_loop(0, 3 * parts, part, 0)


def spread(k2_ref, w2_ref, a, p, rows):
    x, y, z = (k2_ref[a, p, q, rows].astype(F32) * 0.5 for q in range(3))
    even = x + z
    w2_ref[0, a, p, rows] = (even + y).astype(BF16)
    w2_ref[1, a, p, rows] = (even - y).astype(BF16)


def own_kernel(rows_ref, b1_ref, x_ref, cross_ref, chip_ref, k1_ref, wa_ref, xs, hs, wb_ref):
    frames = x_ref.shape[0]
    length = rows_ref[lax.axis_index("tile")]
    assemble(xs, x_ref, cross_ref, chip_ref, 0, length)
    own = hs.shape[1]
    sources = [[(xs, frames - 2 - own + n + a) for a in range(3)] for n in range(own)]
    tasks = [
        functools.partial(fold, k1_ref, wb_ref, 1, a, slice(r, r + CHUNK))
        for a in range(3) for r in range(0, k1_ref.shape[3], CHUNK)
    ]
    first_conv(
        sources, (wa_ref, wb_ref), b1_ref[...], hs, 0, length, (tasks[0::2], tasks[1::2], (), ())
    )


def rest_kernel(
    rows_ref, b1_ref, b2_ref, prev_ref, dcross_ref, dchip_ref, xo, ho, wa_ref, wb_ref, k2_ref, out_hbm, xp, hp, w2_ref, mix, stage, sem
):
    frames, cap, cols, ch = prev_ref.shape
    tile = lax.axis_index("tile")
    length = rows_ref[tile]
    first = [xo[0, i, :, ch:2 * ch] for i in range(cap + 2)]
    assemble(xp, prev_ref, dcross_ref, dchip_ref, 0, length, (lax.axis_index("tm") == 0, first))

    tasks = [
        functools.partial(spread, k2_ref, w2_ref, a, p, slice(r, r + CHUNK))
        for a in range(3) for p in range(3) for r in range(0, k2_ref.shape[3], CHUNK)
    ]
    shared = hp.shape[1]
    source = [(xp, f) for f in range(frames)] + [(xo, f) for f in range(frames)]
    for f in range(0, shared, FIRST_STEP):
        first_conv(
            [[source[f + n + a] for a in range(3)] for n in range(FIRST_STEP)], (wa_ref, wb_ref), b1_ref[...], hp, f,
            length, [tasks[n::2 * shared] for n in range(2 * f, 2 * f + 4)],
        )

    bias_two = b2_ref[...]
    copies = []
    hidden = [(hp, f) for f in range(shared)] + [(ho, f) for f in range(ho.shape[1])]
    for r in range(2):
        rows = ((1, 0), (0, 0), (1, 1)) if r == 0 else ((0, 0), (1, 1), (0, 1))
        m = []
        for c in range(4):
            lhs = jnp.concatenate(
                [
                    jnp.concatenate(
                        [
                            ref[phase, g, k:k + cap, :, c * ch:(c + 1) * ch].reshape(cap * cols, ch)
                            for a in range(3) for phase, k in rows for ref, g in [hidden[f + a]]
                        ],
                        axis=1,
                    )
                    for f in range(frames)
                ],
                axis=0,
            )
            if c in (1, 2):
                taps = w2_ref[c - 1].reshape(9 * ch, ch)
            else:
                taps = jnp.concatenate([k2_ref[a, p, 2 * (c // 3)] for a in range(3) for p in range(3)], axis=0)
            m.append(dot(lhs, taps))
        sums = [
            (v + bias_two).reshape(frames, cap, cols, ch) for v in (m[0] + (m[1] + m[2]), (m[1] - m[2]) - m[3])
        ]
        for f in range(frames):
            for i in range(cap):
                residual = xo[f, i + 1, :, ch:2 * ch].astype(F32)
                keep = i < length
                for c in range(2):
                    value = jnp.where(keep, sums[c][f, i] + residual, 0.0)
                    for part in range(ch // 128):
                        mix[r, f, i, part, pl.ds(c, cols, stride=2), :] = value[:, 128 * part:128 * (part + 1)]
                for part in range(ch // 128):
                    lanes = slice(128 * part, 128 * (part + 1))
                    stage[r, f, i, :, lanes] = mix[r, f, i, part].astype(BF16)
            copies.append(pltpu.make_async_copy(stage.at[r, f], out_hbm.at[f, :, r], sem.at[r, f]))
            copies[-1].start()
    for copy in copies:
        copy.wait()


def in_hbm(value):
    return pltpu.with_memory_space_constraint(value, pltpu.HBM)


def in_vmem(value):
    return pltpu.with_memory_space_constraint(value, pltpu.VMEM)


def local(latent, tile_rows, kernel_one, bias_one, kernel_two, bias_two):
    frames, cap, cols, ch = latent.shape
    groups, tiles = lax.axis_size("tm"), lax.axis_size("tile")
    vmem = pl.BlockSpec(memory_space=pltpu.VMEM)
    smem = pl.BlockSpec(memory_space=pltpu.SMEM)
    hbm = pl.BlockSpec(memory_space=pltpu.HBM)
    bias_one, bias_two = bias_one.reshape(1, ch), bias_two.reshape(1, ch)

    prev = rotated(latent, "tm")
    rim = pltpu.VMEM((frames, 1, cols, ch), BF16)
    to_cross, to_chip = pl.pallas_call(
        pick_kernel,
        out_shape=(rim, rim),
        in_specs=[hbm] * 4,
        out_specs=(vmem, vmem),
        scratch_shapes=[
            pltpu.SMEM(tile_rows.shape, jnp.int32),
            pltpu.VMEM(latent.shape, BF16),
            pltpu.SemaphoreType.DMA((2,)),
        ],
        compiler_params=pltpu.CompilerParams(vmem_limit_bytes=4 << 20),
        cost_estimate=pl.CostEstimate(flops=0, bytes_accessed=1 << 19, transcendentals=0),
        name="pick",
    )(in_hbm(tile_rows), in_hbm(latent), in_hbm(kernel_one), in_hbm(kernel_two))
    chip = lax.ppermute(to_chip, AXES, routes(groups, tiles, 0, "chip"))
    cross = lax.ppermute(to_cross, AXES, routes(groups, tiles, 0, "cross"))
    dcross = lax.ppermute(to_cross, AXES, routes(groups, tiles, 1, "cross"))
    dchip = lax.ppermute(to_chip, AXES, routes(groups, tiles, 1, "chip"))

    kernel_one, kernel_two = in_vmem(kernel_one), in_vmem(kernel_two)
    folded = pltpu.VMEM((2, 3, 2, 2, ch, ch), BF16)
    wa = pl.pallas_call(
        fold_kernel,
        out_shape=folded,
        in_specs=[vmem],
        out_specs=vmem,
        compiler_params=pltpu.CompilerParams(vmem_limit_bytes=4 << 20),
        cost_estimate=pl.CostEstimate(flops=0, bytes_accessed=8 << 20, transcendentals=0),
        name="fold",
    )(kernel_one)
    wa = in_vmem(wa)

    own = frames - 2
    xo, ho, wb = pl.pallas_call(
        own_kernel,
        out_shape=(
            pltpu.VMEM((frames, cap + 2, cols, 3 * ch), BF16),
            pltpu.VMEM((2, own, cap + 1, cols, 4 * ch), BF16),
            folded,
        ),
        in_specs=[smem] + [vmem] * 6,
        out_specs=(vmem, vmem, vmem),
        compiler_params=pltpu.CompilerParams(vmem_limit_bytes=20 << 20),
        cost_estimate=pl.CostEstimate(flops=0, bytes_accessed=8 << 20, transcendentals=0),
        name="own",
    )(tile_rows, bias_one, latent, cross, chip, kernel_one, wa)

    mixed = pl.pallas_call(
        rest_kernel,
        out_shape=jax.ShapeDtypeStruct((frames, cap, 2, 2 * cols, ch), BF16),
        in_specs=[smem] + [vmem] * 10,
        out_specs=hbm,
        scratch_shapes=[
            pltpu.VMEM((frames, cap + 2, cols, 3 * ch), BF16),
            pltpu.VMEM((2, frames, cap + 1, cols, 4 * ch), BF16),
            pltpu.VMEM((2, 3, 3, ch, ch), BF16),
            pltpu.VMEM((2, frames, cap, ch // 128, 2 * cols, 128), F32),
            pltpu.VMEM((2, frames, cap, 2 * cols, ch), BF16),
            pltpu.SemaphoreType.DMA((2, frames)),
        ],
        compiler_params=pltpu.CompilerParams(vmem_limit_bytes=36 << 20),
        cost_estimate=pl.CostEstimate(flops=10 << 30, bytes_accessed=2 << 20, transcendentals=0),
        name="rest",
    )(
        tile_rows, bias_one, bias_two, prev, dcross, dchip,
        in_vmem(xo), in_vmem(ho), wa, in_vmem(wb), kernel_two,
    )
    return mixed.reshape(frames, 2 * cap, 2 * cols, ch)


def solution(mesh):
    in_specs = (P("tm", "tile", None, None), P(), P(), P(), P(), P())
    out_specs = P("tm", "tile", None, None)
    return jax.shard_map(local, mesh=mesh, in_specs=in_specs, out_specs=out_specs, check_vma=False)
```

```python
import functools

import jax
import jax.numpy as jnp
from jax import lax
from jax.experimental import pallas as pl
from jax.experimental.pallas import tpu as pltpu
from jax.sharding import PartitionSpec as P

F32 = jnp.float32
BF16 = jnp.bfloat16
AXES = ("tm", "tile")
FIRST_STEP = 2
CHUNK = 32


def rotated(block, axis):
    count = lax.axis_size(axis)
    return lax.ppermute(block, axis, [(i, (i + 1) % count) for i in range(count)])


def routes(groups, tiles, step, side):
    pairs = []
    for g in range(groups):
        for t in range(tiles):
            if side == "chip":
                to = t ^ 1
            else:
                to = t + 1 if t % 2 else t - 1
            if 0 <= to < tiles:
                pairs.append((g * tiles + t, ((g + step) % groups) * tiles + to))
            else:
                pairs.append((g * tiles + t, g * tiles + tiles - 1 - t))
    return pairs


def down(v):
    n = v.shape[-2]
    ids = lax.broadcasted_iota(jnp.int32, v.shape, v.ndim - 2)
    return jnp.where(ids == 0, 0.0, pltpu.roll(v, 1, v.ndim - 2))


def up(v):
    n = v.shape[-2]
    ids = lax.broadcasted_iota(jnp.int32, v.shape, v.ndim - 2)
    return jnp.where(ids == n - 1, 0.0, pltpu.roll(v, n - 1, v.ndim - 2))


def pick_kernel(rows_hbm, x_hbm, _, __, cross_ref, chip_ref, rows_ref, x_ref, sem):
    copies = [
        pltpu.make_async_copy(rows_hbm, rows_ref, sem.at[0]),
        pltpu.make_async_copy(x_hbm, x_ref, sem.at[1]),
    ]
    for copy in copies:
        copy.start()
    for copy in copies:
        copy.wait()
    tile = lax.axis_index("tile")
    last = rows_ref[tile] - 1
    odd = lax.rem(tile, 2) == 1
    cross_ref[:, 0] = x_ref[:, jnp.where(odd, last, 0)]
    chip_ref[:, 0] = x_ref[:, jnp.where(odd, 0, last)]


def assemble(xs, own, cross_ref, chip_ref, chip_row, length, which, instead=None):
    _, cap, cols, ch = own.shape
    tile = lax.axis_index("tile")
    odd = lax.rem(tile, 2) == 1
    has_cross = jnp.logical_and(tile > 0, tile < lax.axis_size("tile") - 1)
    for f in which:
        cross = jnp.where(has_cross, cross_ref[f, 0], jnp.zeros((cols, ch), BF16))
        chip = chip_ref[f, chip_row]
        below = jnp.where(odd, cross, chip)
        rows = [jnp.where(odd, chip, cross), own[f, 0]]
        rows += [jnp.where(length == i, below, own[f, i]) for i in range(1, cap)] + [below]
        for i, z in enumerate(rows):
            if instead is not None:
                z = jnp.where(instead[0], instead[1][i], z)
            wide = z.astype(F32)
            xs[f, i, :, 0:ch] = down(wide).astype(BF16)
            xs[f, i, :, ch:2 * ch] = z
            xs[f, i, :, 2 * ch:3 * ch] = up(wide).astype(BF16)


def dot(lhs, rhs):
    return jnp.dot(lhs, rhs, preferred_element_type=F32)


def first_conv(sources, weights, bias, hs, f, length, beside):
    n = len(sources)
    _, _, half, cols, wide = hs.shape
    ch = wide // 4
    tile = lax.axis_index("tile")
    top = tile == 0
    bottom = tile == lax.axis_size("tile") - 1
    for phase in range(2):
        act = []
        for c in range(2):
            lhs = jnp.concatenate(
                [
                    jnp.concatenate(
                        [
                            ref[g, i:i + half, :, c * ch:(c + 2) * ch].reshape(half * cols, 2 * ch)
                            for a in range(3) for i in range(2) for ref, g in [taps[a]]
                        ],
                        axis=1,
                    )
                    for taps in sources
                ],
                axis=0,
            )
            v = dot(lhs, weights[phase][c].reshape(12 * ch, ch)) + bias
            for task in beside[2 * phase + c]:
                task()
            v = v / (1.0 + jnp.exp(-v))
            act.append(v.reshape(n, half, cols, ch))
        he, ho = act
        k = lax.broadcasted_iota(jnp.int32, he.shape, 1)
        if phase == 0:
            keep = jnp.logical_not(jnp.logical_and(bottom, k == length))
        else:
            keep = jnp.logical_not(jnp.logical_and(top, k == 0))
        he = jnp.where(keep, he, 0.0)
        ho = jnp.where(keep, ho, 0.0)
        for c, value in enumerate((down(ho) - ho, he + ho, ho - he, he - up(he))):
            hs[phase, f:f + n, :, :, c * ch:(c + 1) * ch] = value.astype(BF16)


def fold(k1_ref, w_ref, phase, a, rows):
    def pairs(x, y, z):
        return (x, y + z), (x + y, z)

    g = [[k1_ref[a, p, q, rows].astype(F32) for q in range(3)] for p in range(3)]
    by_row = [pairs(g[0][q], g[1][q], g[2][q])[phase] for q in range(3)]
    for i in range(2):
        taps = pairs(by_row[0][i], by_row[1][i], by_row[2][i])
        for c in range(2):
            for j in range(2):
                if i == phase and c == j:
                    w_ref[c, a, i, j, rows] = k1_ref[a, 2 * i, 2 * j, rows]
                else:
                    w_ref[c, a, i, j, rows] = taps[c][j].astype(BF16)


def fold_kernel(k1_ref, w_ref):
    parts = k1_ref.shape[3] // CHUNK

    def part(s, _):
        fold(k1_ref, w_ref, 0, s // parts, pl.ds(pl.multiple_of(lax.rem(s, parts) * CHUNK, CHUNK), CHUNK))
        return 0

    lax.fori_loop(0, 3 * parts, part, 0)


def spread(k2_ref, w2_ref, a, p, rows):
    x, y, z = (k2_ref[a, p, q, rows].astype(F32) * 0.5 for q in range(3))
    even = x + z
    w2_ref[0, a, p, rows] = (even + y).astype(BF16)
    w2_ref[1, a, p, rows] = (even - y).astype(BF16)


def own_kernel(rows_ref, b1_ref, x_ref, cross_ref, chip_ref, k1_ref, wa_ref, xs, hs, wb_ref):
    frames = x_ref.shape[0]
    length = rows_ref[lax.axis_index("tile")]
    assemble(xs, x_ref, cross_ref, chip_ref, 0, length, range(frames))
    own = hs.shape[1]
    sources = [[(xs, frames - 2 - own + n + a) for a in range(3)] for n in range(own)]
    tasks = [
        functools.partial(fold, k1_ref, wb_ref, 1, a, slice(r, r + CHUNK))
        for a in range(3) for r in range(0, k1_ref.shape[3], CHUNK)
    ]
    first_conv(
        sources, (wa_ref, wb_ref), b1_ref[...], hs, 0, length, (tasks[0::2], tasks[1::2], (), ())
    )


def rest_kernel(
    rows_ref, b1_ref, b2_ref, prev_ref, dcross_ref, dchip_ref, xo, ho, wa_ref, wb_ref, k2_ref, out_hbm, xp, hp, w2_ref, mix, stage, sem
):
    frames, cap, cols, ch = prev_ref.shape
    tile = lax.axis_index("tile")
    length = rows_ref[tile]
    first = [xo[0, i, :, ch:2 * ch] for i in range(cap + 2)]
    earlier = functools.partial(assemble, xp, prev_ref, dcross_ref, dchip_ref, 0, length)
    instead = (lax.axis_index("tm") == 0, first)
    earlier(range(frames - FIRST_STEP, frames), instead)
    tasks = [
        functools.partial(spread, k2_ref, w2_ref, a, p, slice(r, r + CHUNK))
        for a in range(3) for p in range(3) for r in range(0, k2_ref.shape[3], CHUNK)
    ]
    shared = hp.shape[1]
    source = [(xp, f) for f in range(frames)] + [(xo, f) for f in range(frames)]
    for f in reversed(range(0, shared, FIRST_STEP)):
        beside = [tasks[n::2 * shared] for n in range(2 * f, 2 * f + 4)]
        if f:
            beside[0] = [functools.partial(earlier, range(f - FIRST_STEP, f), instead)] + beside[0]
        first_conv(
            [[source[f + n + a] for a in range(3)] for n in range(FIRST_STEP)], (wa_ref, wb_ref), b1_ref[...], hp, f,
            length, beside,
        )

    bias_two = b2_ref[...]
    copies = []
    hidden = [(hp, f) for f in range(shared)] + [(ho, f) for f in range(ho.shape[1])]
    for r in range(2):
        rows = ((1, 0), (0, 0), (1, 1)) if r == 0 else ((0, 0), (1, 1), (0, 1))
        m = []
        for c in range(4):
            lhs = jnp.concatenate(
                [
                    jnp.concatenate(
                        [
                            ref[phase, g, k:k + cap, :, c * ch:(c + 1) * ch].reshape(cap * cols, ch)
                            for a in range(3) for phase, k in rows for ref, g in [hidden[f + a]]
                        ],
                        axis=1,
                    )
                    for f in range(frames)
                ],
                axis=0,
            )
            if c in (1, 2):
                taps = w2_ref[c - 1].reshape(9 * ch, ch)
            else:
                taps = jnp.concatenate([k2_ref[a, p, 2 * (c // 3)] for a in range(3) for p in range(3)], axis=0)
            m.append(dot(lhs, taps))
        sums = [
            (v + bias_two).reshape(frames, cap, cols, ch) for v in (m[0] + (m[1] + m[2]), (m[1] - m[2]) - m[3])
        ]
        for f in range(frames):
            for i in range(cap):
                residual = xo[f, i + 1, :, ch:2 * ch].astype(F32)
                keep = i < length
                for c in range(2):
                    value = jnp.where(keep, sums[c][f, i] + residual, 0.0)
                    for part in range(ch // 128):
                        mix[r, f, i, part, pl.ds(c, cols, stride=2), :] = value[:, 128 * part:128 * (part + 1)]
                for part in range(ch // 128):
                    lanes = slice(128 * part, 128 * (part + 1))
                    stage[r, f, i, :, lanes] = mix[r, f, i, part].astype(BF16)
            copies.append(pltpu.make_async_copy(stage.at[r, f], out_hbm.at[f, :, r], sem.at[r, f]))
            copies[-1].start()
    for copy in copies:
        copy.wait()


def in_hbm(value):
    return pltpu.with_memory_space_constraint(value, pltpu.HBM)


def in_vmem(value):
    return pltpu.with_memory_space_constraint(value, pltpu.VMEM)


def local(latent, tile_rows, kernel_one, bias_one, kernel_two, bias_two):
    frames, cap, cols, ch = latent.shape
    groups, tiles = lax.axis_size("tm"), lax.axis_size("tile")
    vmem = pl.BlockSpec(memory_space=pltpu.VMEM)
    smem = pl.BlockSpec(memory_space=pltpu.SMEM)
    hbm = pl.BlockSpec(memory_space=pltpu.HBM)
    bias_one, bias_two = bias_one.reshape(1, ch), bias_two.reshape(1, ch)

    prev = rotated(latent, "tm")
    rim = pltpu.VMEM((frames, 1, cols, ch), BF16)
    to_cross, to_chip = pl.pallas_call(
        pick_kernel,
        out_shape=(rim, rim),
        in_specs=[hbm] * 4,
        out_specs=(vmem, vmem),
        scratch_shapes=[
            pltpu.SMEM(tile_rows.shape, jnp.int32),
            pltpu.VMEM(latent.shape, BF16),
            pltpu.SemaphoreType.DMA((2,)),
        ],
        compiler_params=pltpu.CompilerParams(vmem_limit_bytes=4 << 20),
        cost_estimate=pl.CostEstimate(flops=0, bytes_accessed=1 << 19, transcendentals=0),
        name="pick",
    )(in_hbm(tile_rows), in_hbm(latent), in_hbm(kernel_one), in_hbm(kernel_two))
    chip = lax.ppermute(to_chip, AXES, routes(groups, tiles, 0, "chip"))
    cross = lax.ppermute(to_cross, AXES, routes(groups, tiles, 0, "cross"))
    dcross = lax.ppermute(to_cross, AXES, routes(groups, tiles, 1, "cross"))
    dchip = lax.ppermute(to_chip, AXES, routes(groups, tiles, 1, "chip"))

    kernel_one, kernel_two = in_vmem(kernel_one), in_vmem(kernel_two)
    folded = pltpu.VMEM((2, 3, 2, 2, ch, ch), BF16)
    wa = pl.pallas_call(
        fold_kernel,
        out_shape=folded,
        in_specs=[vmem],
        out_specs=vmem,
        compiler_params=pltpu.CompilerParams(vmem_limit_bytes=4 << 20),
        cost_estimate=pl.CostEstimate(flops=0, bytes_accessed=8 << 20, transcendentals=0),
        name="fold",
    )(kernel_one)
    wa = in_vmem(wa)

    own = frames - 2
    xo, ho, wb = pl.pallas_call(
        own_kernel,
        out_shape=(
            pltpu.VMEM((frames, cap + 2, cols, 3 * ch), BF16),
            pltpu.VMEM((2, own, cap + 1, cols, 4 * ch), BF16),
            folded,
        ),
        in_specs=[smem] + [vmem] * 6,
        out_specs=(vmem, vmem, vmem),
        compiler_params=pltpu.CompilerParams(vmem_limit_bytes=20 << 20),
        cost_estimate=pl.CostEstimate(flops=0, bytes_accessed=8 << 20, transcendentals=0),
        name="own",
    )(tile_rows, bias_one, latent, cross, chip, kernel_one, wa)

    mixed = pl.pallas_call(
        rest_kernel,
        out_shape=jax.ShapeDtypeStruct((frames, cap, 2, 2 * cols, ch), BF16),
        in_specs=[smem] + [vmem] * 10,
        out_specs=hbm,
        scratch_shapes=[
            pltpu.VMEM((frames, cap + 2, cols, 3 * ch), BF16),
            pltpu.VMEM((2, frames, cap + 1, cols, 4 * ch), BF16),
            pltpu.VMEM((2, 3, 3, ch, ch), BF16),
            pltpu.VMEM((2, frames, cap, ch // 128, 2 * cols, 128), F32),
            pltpu.VMEM((2, frames, cap, 2 * cols, ch), BF16),
            pltpu.SemaphoreType.DMA((2, frames)),
        ],
        compiler_params=pltpu.CompilerParams(vmem_limit_bytes=36 << 20),
        cost_estimate=pl.CostEstimate(flops=10 << 30, bytes_accessed=2 << 20, transcendentals=0),
        name="rest",
    )(
        tile_rows, bias_one, bias_two, prev, dcross, dchip,
        in_vmem(xo), in_vmem(ho), wa, in_vmem(wb), kernel_two,
    )
    return mixed.reshape(frames, 2 * cap, 2 * cols, ch)


def solution(mesh):
    in_specs = (P("tm", "tile", None, None), P(), P(), P(), P(), P())
    out_specs = P("tm", "tile", None, None)
    return jax.shard_map(local, mesh=mesh, in_specs=in_specs, out_specs=out_specs, check_vma=False)
```
